32 devices in a mesh: ctx: 4 (over z), ch: 8 (over y, x, core).
Axes of the slice: x: 2, y: 2, z: 4, core: 2. Of those that a mesh axis runs over, the one named last changes fastest.
Arguments:
- features: bfloat16 [3, 1024, 8192], P(None, 'ctx', 'ch'), may hold values from -6 to 6
- short_weight: float32 [3, 7, 8192], P(None, None, 'ch'), may hold values from -2 to 2
- rates: float32 [8192, 16], P('ch'), may hold values from 0.00029296876 to 0.08
- residues: float32 [8192, 16], P('ch'), may hold values from -0.75 to 0.75
- skip: float32 [8192], P('ch'), may hold values from -4 to 4
- out_weight: bfloat16 [8192, 8192], P('ctx', 'ch'), may hold values from -0.0625 to 0.0625
Outputs:
- mixed: bfloat16 [1024, 8192], P('ctx', 'ch')
The draws below stay inside these ranges and needn't reach their ends.
All inputs are finite; a program needn't handle non-finite values.
Results may differ from the reference program's by a relative error of at most 0.0076.
Values may be sent and summed in bfloat16 or wider, within the bound.
A program may use at most 128 MiB of HBM per device.

```python
import math
import jax
import jax.numpy as jnp
from jax import lax

D = 8192
MODES = 16
WIDTH = 7
TOKENS = 1024


def block_levels(own_key, extent, cuts, least, top_value):
    def one(dim, blocks):
        heights = jax.random.uniform(jax.random.fold_in(jax.random.fold_in(own_key, 6), dim), (blocks,), jnp.float32, least / len(cuts), top_value / len(cuts))
        return jnp.repeat(jnp.exp(heights), extent[dim] // blocks).reshape((-1,) + (1,) * (len(extent) - dim - 1))

    gain = one(*cuts[0])
    for cut in cuts[1:]:
        gain = gain * one(*cut)
    return gain


def noise(key, dims, deviation, limit, shards=(), kind=jnp.bfloat16):
    factor_of = block_levels(key, dims, shards, -0.22, 0.18) if shards else 1.0
    result = jax.random.normal(key, dims, jnp.float32) * deviation * factor_of
    return jnp.minimum(jnp.maximum(result, -limit), limit).astype(kind)


def setup_inputs(seed: int = 0) -> dict:
    splits = jax.random.split(jax.random.key(seed), 7)
    features = noise(splits[0], (3, TOKENS, D), 1.0, 6.0, ((1, 4), (2, 8)))
    short_weight = noise(splits[1], (3, WIDTH, D), WIDTH ** -0.5, 2.0, ((2, 8),), jnp.float32)
    rates = jnp.clip(jnp.exp(math.log(0.08) - 5.609716 * jax.random.uniform(splits[2], (D, MODES), jnp.float32) ** block_levels(splits[2], (D, MODES), ((0, 8),), -0.2, 0.2)), 0.00029296876, 0.08)
    residues = noise(splits[3], (D, MODES), 0.05, 0.75, ((0, 8),), jnp.float32)
    skip = noise(splits[4], (D,), 1.0, 4.0, ((0, 8),), jnp.float32)
    out_weight = noise(splits[5], (D, D), D ** -0.5, 0.0625, ((0, 4), (1, 8)))
    return dict(features=features, short_weight=short_weight, rates=rates, residues=residues, skip=skip, out_weight=out_weight)


def reference(features, short_weight, rates, residues, skip, out_weight):
    inputs = features.astype(jnp.float32)
    padded = jnp.pad(inputs, ((0, 0), (WIDTH - 1, 0), (0, 0)))
    featured = jnp.zeros_like(inputs)
    for offset in range(WIDTH):
        featured = featured + short_weight[:, offset][:, None, :] * padded[:, WIDTH - 1 - offset:WIDTH - 1 - offset + TOKENS, :]
    featured = featured.astype(jnp.bfloat16)
    query = featured[0].astype(jnp.float32)
    product = (featured[1].astype(jnp.float32) * featured[2].astype(jnp.float32)).astype(jnp.bfloat16)
    product_value = product.astype(jnp.float32)
    group_size = math.gcd(D, 256)
    group_count = D // group_size
    positions = jnp.arange(TOKENS, dtype=jnp.float32)
    fft_length = 2 * TOKENS

    def convolve(block):
        rate_block, gain_block, signal = block
        kernel = jnp.einsum("cn,cnt->ct", gain_block, jnp.exp(-rate_block[:, :, None] * positions[None, None, :]), precision=lax.Precision.HIGHEST)
        spectrum = jnp.fft.rfft(signal.T, n=fft_length) * jnp.fft.rfft(kernel, n=fft_length)
        return jnp.fft.irfft(spectrum, n=fft_length)[:, :TOKENS].T

    signals = product_value.reshape(TOKENS, group_count, group_size).transpose(1, 0, 2)
    convolved = lax.map(convolve, (rates.reshape(group_count, group_size, MODES), residues.reshape(group_count, group_size, MODES), signals))
    convolved = convolved.transpose(1, 0, 2).reshape(TOKENS, D)
    conv_value = convolved + skip[None, :] * product_value
    gated = (query * conv_value).astype(jnp.bfloat16)
    return jnp.dot(gated, out_weight, preferred_element_type=jnp.float32).astype(jnp.bfloat16)
```

```python
import functools
import jax
import jax.numpy as jnp
from jax import lax
from jax.experimental import pallas as pl
from jax.experimental.pallas import tpu as pltpu
from jax.sharding import PartitionSpec as P

MESH = pl.DeviceIdType.MESH
LANES = 128
HEAD = 8
RIM = 16
UNROLL = 8


def each(low, high, body):
    if high - low <= 8:
        for i in range(low, high):
            body(i)
    else:

        def step(i, carry):
            body(i)
            return carry

        lax.fori_loop(low, high, step, 0)


def remote(src, dst, send_sem, recv_sem, device):
    return pltpu.make_async_remote_copy(
        src_ref=src,
        dst_ref=dst,
        send_sem=send_sem,
        recv_sem=recv_sem,
        device_id=device,
        device_id_type=MESH,
    )


def rounded(value):
    return value.astype(jnp.bfloat16).astype(jnp.float32)


def added(terms):
    while len(terms) > 1:
        terms = [a + b for a, b in zip(terms[::2], terms[1::2])] + (
            [terms[-1]] if len(terms) % 2 else []
        )
    return terms[0]


def operator_kernel(
    nz, modes, width,
    feat_ref, taps_ref, rates_ref, gains_ref, skip_ref,
    out_ref,
    rim, wide, product, query, gated, total, states,
    rim_send, rim_recv, state_send, state_recv,
):
    z, c = lax.axis_index("ctx"), lax.axis_index("ch")
    tokens, chans = feat_ref.shape[1], feat_ref.shape[2]
    subs = chans // LANES
    parts, rows = out_ref.shape[0], out_ref.shape[1]

    barrier = pltpu.get_barrier_semaphore()

    def greet(d):
        pl.semaphore_signal(
            barrier, inc=1, device_id=(lax.rem(z + d, nz), c), device_id_type=MESH
        )

    each(1, nz, greet)
    pl.semaphore_wait(barrier, nz - 1)

    rim_copy = remote(
        feat_ref.at[:, pl.ds(tokens - RIM, RIM), :], rim, rim_send, rim_recv,
        (lax.rem(z + 1, nz), c),
    )

    @pl.when(z < nz - 1)
    def _():
        rim_copy.start()

    for s in range(3):
        for g in range(subs):
            wide[s, pl.ds(HEAD * subs + g, tokens, stride=subs), :] = feat_ref[
                s, :, g * LANES : (g + 1) * LANES
            ].astype(jnp.float32)

    @pl.when(z > 0)
    def _():
        rim_copy.wait_recv()
        for s in range(3):
            for g in range(subs):
                part = rim[s, :, g * LANES : (g + 1) * LANES].astype(jnp.float32)
                wide[s, pl.ds(g, HEAD, stride=subs), :] = part[RIM - HEAD :, :]

    @pl.when(z == 0)
    def _():
        wide[:, pl.ds(0, HEAD * subs), :] = jnp.zeros((3, HEAD * subs, LANES), jnp.float32)

    def at(n):
        return pl.ds(n * subs, subs)

    def token(t):
        return pl.ds(pl.multiple_of(t * subs, subs), subs)

    def featured(s, t, weights):
        value = weights[0] * wide[s, token(t + HEAD), :]
        for j in range(1, width):
            value = value + weights[j] * wide[s, token(t + HEAD - j), :]
        return rounded(value)

    def taps_of(s):
        return [taps_ref[at(s * width + j), :] for j in range(width)]

    decay = [jnp.exp(-rates_ref[at(n), :]) for n in range(modes)]
    taps_1, taps_2 = taps_of(1), taps_of(2)

    def first(i, carry):
        carry = list(carry)
        for u in range(UNROLL):
            t = i * UNROLL + u
            value = rounded(featured(1, t, taps_1) * featured(2, t, taps_2))
            product[token(t), :] = value
            carry = [k * m + value for k, m in zip(decay, carry)]
        return tuple(carry)

    zero = jnp.zeros((subs, LANES), jnp.float32)
    ends = lax.fori_loop(0, tokens // UNROLL, first, (zero,) * modes)
    for n in range(modes):
        total[at(n), :] = ends[n]

    def pass_on(d):
        @pl.when(z + d < nz)
        def _():
            remote(
                total, states.at[d - 1], state_send.at[d - 1], state_recv.at[d - 1],
                (lax.rem(z + d, nz), c),
            ).start()

    each(1, nz, pass_on)

    taps_0 = taps_of(0)

    def second(i, carry):
        for u in range(UNROLL):
            t = i * UNROLL + u
            query[token(t), :] = featured(0, t, taps_0)
        return carry

    lax.fori_loop(0, tokens // UNROLL, second, 0)

    def arrive(d):
        @pl.when(z >= d)
        def _():
            remote(
                total, states.at[d - 1], state_send.at[d - 1], state_recv.at[d - 1],
                (lax.rem(z + d, nz), c),
            ).wait_recv()

        @pl.when(z < d)
        def _():
            states[d - 1] = jnp.zeros((modes * subs, LANES), jnp.float32)

    each(1, nz, arrive)

    incoming = []
    for n in range(modes):
        span = jnp.exp(-rates_ref[at(n), :] * float(tokens))
        value = states[nz - 2, at(n), :]
        for d in range(nz - 2, 0, -1):
            value = value * span + states[d - 1, at(n), :]
        incoming.append(value)

    gains = [gains_ref[at(n), :] for n in range(modes)]
    skip = skip_ref[...]

    def third(i, carry):
        carry = list(carry)
        for u in range(UNROLL):
            t = i * UNROLL + u
            value = product[token(t), :]
            carry = [k * m + value for k, m in zip(decay, carry)]
            conv = added([g * m for g, m in zip(gains, carry)] + [skip * value])
            gated[token(t), :] = query[token(t), :] * conv
        return tuple(carry)

    lax.fori_loop(0, tokens // UNROLL, third, tuple(incoming))

    for j in range(parts):
        for g in range(subs):
            out_ref[j, :, g * LANES : (g + 1) * LANES] = gated[
                pl.ds(j * rows * subs + g, rows, stride=subs), :
            ].astype(jnp.bfloat16)

    @pl.when(z < nz - 1)
    def _():
        rim_copy.wait_send()

    def leave(d):
        @pl.when(z + d < nz)
        def _():
            remote(
                total, states.at[d - 1], state_send.at[d - 1], state_recv.at[d - 1],
                (lax.rem(z + d, nz), c),
            ).wait_send()

    each(1, nz, leave)


def project_kernel(
    nz, nc,
    g_ref, w_ref,
    out_ref,
    weights, stage, blocks, sent, taken, own,
    w_sem, a_send, a_recv, b_send, b_recv, s_send, s_recv, m_send, m_recv, p_send, p_recv,
):
    z, c = lax.axis_index("ctx"), lax.axis_index("ch")
    fold = nc // nz
    chips = nc // 2
    chip, core = c // 2, lax.rem(c, 2)
    mate = c + 1 - 2 * core
    tokens, columns = out_ref.shape
    rows, chans = g_ref.shape[1], g_ref.shape[2]
    tile = min(columns, 256)

    barrier = pltpu.get_barrier_semaphore()

    def greet_plane(i):
        pl.semaphore_signal(
            barrier, inc=1, device_id=(z, lax.rem(c + i, nc)), device_id_type=MESH
        )

    def greet_line(d):
        pl.semaphore_signal(
            barrier, inc=1, device_id=(lax.rem(z + d, nz), c), device_id_type=MESH
        )

    each(1, nc, greet_plane)
    each(1, nz, greet_line)
    pl.semaphore_wait(barrier, nc + nz - 2)

    w_copy = pltpu.make_async_copy(w_ref, weights, w_sem)

    def scatter(i):
        j = lax.rem(c + i, nc)
        return remote(g_ref.at[j], stage.at[c], a_send.at[i], a_recv.at[c], (z, j))

    each(1, nc, lambda i: scatter(i).start())
    own_part = pltpu.make_async_copy(g_ref.at[c], stage.at[c], a_recv.at[c])
    own_part.start()
    w_copy.start()

    def plane(d):
        return lax.rem(z + d, nz)

    def along(d):
        q = plane(d)
        src = stage.at[pl.ds(q * fold, fold)]
        dst = blocks.at[z, :, c]
        if d == nz:
            return pltpu.make_async_copy(src, dst, b_recv.at[z])
        return remote(src, dst, b_send.at[d], b_recv.at[z], (q, c))

    for d in range(1, nz + 1):
        for m in range(fold):
            k = plane(d) * fold + m
            pltpu.make_async_copy(g_ref.at[0], stage.at[k], a_recv.at[k]).wait()
        along(d).start()

    def piece(k, j):
        return blocks.at[k, :, j]

    def spread(d, i):
        k = plane(d)
        to = lax.rem(chip + i, chips) * 2 + core
        return remote(piece(k, c), piece(k, c), s_send.at[d - 1, i], s_recv.at[k, chip], (z, to))

    def hand(d, i):
        k = plane(d)
        p = lax.rem(chip + i, chips)
        j = p * 2 + core
        return remote(piece(k, j), piece(k, j), m_send.at[d - 1, i], m_recv.at[k, p], (z, mate))

    def back(d):
        return remote(
            sent.at[d - 1], taken.at[d - 1], p_send.at[d - 1], p_recv.at[d - 1], (plane(d), c)
        )

    def multiply(d):
        k = plane(d)

        def strip(i):
            cols = pl.ds(pl.multiple_of(i * tile, tile), tile)
            value = jnp.zeros((tokens, tile), jnp.float32)
            for m in range(fold):
                left = blocks[k, m]
                if rows % 16:
                    left = left.astype(jnp.float32).reshape(tokens, chans).astype(jnp.bfloat16)
                else:
                    left = left.reshape(tokens, chans)
                value = value + jnp.dot(
                    left,
                    weights[m * chans : (m + 1) * chans, cols],
                    preferred_element_type=jnp.float32,
                )
            if d == nz:
                own[:, cols] = value
            else:
                sent[d - 1, :, cols] = value.astype(jnp.bfloat16)

        pl.loop(0, columns // tile)(strip)

    for step in range(nz + 2):
        if step < nz:
            d = step + 1
            k = plane(d)
            pltpu.make_async_copy(piece(k, c), piece(k, c), b_recv.at[k]).wait()
            each(1, chips, lambda i: spread(d, i).start())
            hand(d, 0).start()
        if 1 <= step <= nz:
            d = step

            def forward(i):
                k = plane(d)
                p = lax.rem(chip + i, chips)
                remote(
                    piece(k, c), piece(k, p * 2 + core), s_send.at[d - 1, i], s_recv.at[k, p], (z, mate)
                ).wait_recv()
                hand(d, i).start()

            each(1, chips, forward)
        if step >= 2:
            d = step - 1

            def collect(i):
                k = plane(d)
                p = lax.rem(chip + i, chips)
                remote(
                    piece(k, c), piece(k, p * 2 + 1 - core), m_send.at[d - 1, i], m_recv.at[k, p], (z, mate)
                ).wait_recv()

            each(0, chips, collect)
            if step == 2:
                w_copy.wait()
            multiply(d)
            if d < nz:
                back(d).start()

    for d in range(1, nz):
        back(d).wait_recv()

    def finish(i):
        span = pl.ds(pl.multiple_of(i * 32, 32), 32)
        value = own[span, :]
        for d in range(1, nz):
            value = value + taken[d - 1, span, :].astype(jnp.float32)
        out_ref[span, :] = value.astype(jnp.bfloat16)

    pl.loop(0, tokens // 32)(finish)

    each(1, nc, lambda i: scatter(i).wait_send())
    for d in range(1, nz):
        along(d).wait_send()
        back(d).wait_send()
    for d in range(1, nz + 1):
        each(1, chips, lambda i: spread(d, i).wait_send())
        each(0, chips, lambda i: hand(d, i).wait_send())


def per_device(nz, nc, features, short_weight, rates, residues, skip, out_weight):
    width = short_weight.shape[1]
    _, tokens, chans = features.shape
    modes = rates.shape[1]
    depth, columns = out_weight.shape
    subs = chans // LANES
    rows = tokens // nc
    fold = nc // nz
    chips = nc // 2
    f32, bf16 = jnp.float32, jnp.bfloat16
    vmem = pl.BlockSpec(memory_space=pltpu.VMEM)
    dma = pltpu.SemaphoreType.DMA

    gated = pl.pallas_call(
        functools.partial(operator_kernel, nz, modes, width),
        out_shape=jax.ShapeDtypeStruct((nc, rows, chans), bf16),
        in_specs=[vmem] * 5,
        out_specs=vmem,
        scratch_shapes=[
            pltpu.VMEM((3, RIM, chans), bf16),
            pltpu.VMEM((3, (tokens + HEAD) * subs, LANES), f32),
            pltpu.VMEM((tokens * subs, LANES), f32),
            pltpu.VMEM((tokens * subs, LANES), f32),
            pltpu.VMEM((tokens * subs, LANES), f32),
            pltpu.VMEM((modes * subs, LANES), f32),
            pltpu.VMEM((nz - 1, modes * subs, LANES), f32),
            dma, dma, dma((nz - 1,)), dma((nz - 1,)),
        ],
        compiler_params=pltpu.CompilerParams(
            collective_id=0, has_side_effects=True, vmem_limit_bytes=40 * 2**20
        ),
        name="operator",
    )(
        features,
        short_weight.reshape(3 * width * subs, LANES),
        rates.T.reshape(modes * subs, LANES),
        residues.T.reshape(modes * subs, LANES),
        skip.reshape(subs, LANES),
    )

    return pl.pallas_call(
        functools.partial(project_kernel, nz, nc),
        out_shape=jax.ShapeDtypeStruct((tokens, columns), bf16),
        in_specs=[vmem, pl.BlockSpec(memory_space=pl.ANY)],
        out_specs=vmem,
        scratch_shapes=[
            pltpu.VMEM((depth, columns), bf16),
            pltpu.VMEM((nc, rows, chans), bf16),
            pltpu.VMEM((nz, fold, nc, rows, chans), bf16),
            pltpu.VMEM((nz - 1, tokens, columns), bf16),
            pltpu.VMEM((nz - 1, tokens, columns), bf16),
            pltpu.VMEM((tokens, columns), f32),
            dma,
            dma((nc,)), dma((nc,)),
            dma((nz,)), dma((nz,)),
            dma((nz, chips)), dma((nz, chips)),
            dma((nz, chips)), dma((nz, chips)),
            dma((nz - 1,)), dma((nz - 1,)),
        ],
        compiler_params=pltpu.CompilerParams(
            collective_id=1, has_side_effects=True, vmem_limit_bytes=40 * 2**20
        ),
        name="project",
    )(gated, out_weight)


def solution(mesh):
    return jax.shard_map(
        functools.partial(per_device, mesh.shape["ctx"], mesh.shape["ch"]),
        mesh=mesh,
        in_specs=(
            P(None, "ctx", "ch"),
            P(None, None, "ch"),
            P("ch", None),
            P("ch", None),
            P("ch"),
            P("ctx", "ch"),
        ),
        out_specs=P("ctx", "ch"),
        check_vma=False,
    )
```

```python
import functools
import jax
import jax.numpy as jnp
from jax import lax
from jax.experimental import pallas as pl
from jax.experimental.pallas import tpu as pltpu
from jax.sharding import PartitionSpec as P

MESH = pl.DeviceIdType.MESH
LANES = 128
HEAD = 8
RIM = 16
UNROLL = 8
CHUNKS = 2


def each(low, high, body):
    if high - low <= 8:
        for i in range(low, high):
            body(i)
    else:

        def step(i, carry):
            body(i)
            return carry

        lax.fori_loop(low, high, step, 0)


def remote(src, dst, send_sem, recv_sem, device):
    return pltpu.make_async_remote_copy(
        src_ref=src,
        dst_ref=dst,
        send_sem=send_sem,
        recv_sem=recv_sem,
        device_id=device,
        device_id_type=MESH,
    )


def rounded(value):
    return value.astype(jnp.bfloat16).astype(jnp.float32)


def added(terms):
    while len(terms) > 1:
        terms = [a + b for a, b in zip(terms[::2], terms[1::2])] + (
            [terms[-1]] if len(terms) % 2 else []
        )
    return terms[0]


def operator_kernel(
    nz, modes, width,
    feat_hbm, taps_in, rates_in, gains_in, skip_ref,
    out_ref,
    feat_ref, taps_ref, rates_ref, gains_ref,
    rim, wide, product, query, gated, total, states,
    feat_sem, rim_send, rim_recv, state_send, state_recv,
):
    z, c = lax.axis_index("ctx"), lax.axis_index("ch")
    tokens, chans = feat_hbm.shape[1], feat_hbm.shape[2]
    subs = chans // LANES
    parts, rows = out_ref.shape[0], out_ref.shape[1]

    def load(s):
        return pltpu.make_async_copy(feat_hbm.at[s], feat_ref.at[s], feat_sem.at[s])

    for s in (1, 2, 0):
        load(s).start()

    barrier = pltpu.get_barrier_semaphore()

    def greet(d):
        pl.semaphore_signal(
            barrier, inc=1, device_id=(lax.rem(z + d, nz), c), device_id_type=MESH
        )

    each(1, nz, greet)

    for g in range(subs):
        lanes = slice(g * LANES, (g + 1) * LANES)
        rates_ref[pl.ds(g, modes, stride=subs), :] = rates_in[:, lanes]
        gains_ref[pl.ds(g, modes, stride=subs), :] = gains_in[:, lanes]
        for s in range(3):
            taps_ref[pl.ds(s * width * subs + g, width, stride=subs), :] = taps_in[s, :, lanes]

    pl.semaphore_wait(barrier, nz - 1)

    rim_copy = remote(
        feat_hbm.at[:, pl.ds(tokens - RIM, RIM), :], rim, rim_send, rim_recv,
        (lax.rem(z + 1, nz), c),
    )

    @pl.when(z < nz - 1)
    def _():
        rim_copy.start()

    def unpack(s):
        load(s).wait()
        for g in range(subs):
            wide[s, pl.ds(HEAD * subs + g, tokens, stride=subs), :] = feat_ref[
                s, :, g * LANES : (g + 1) * LANES
            ].astype(jnp.float32)

    unpack(1)
    unpack(2)

    @pl.when(z > 0)
    def _():
        rim_copy.wait_recv()
        for s in range(3):
            for g in range(subs):
                part = rim[s, :, g * LANES : (g + 1) * LANES].astype(jnp.float32)
                wide[s, pl.ds(g, HEAD, stride=subs), :] = part[RIM - HEAD :, :]

    @pl.when(z == 0)
    def _():
        wide[:, pl.ds(0, HEAD * subs), :] = jnp.zeros((3, HEAD * subs, LANES), jnp.float32)

    def at(n):
        return pl.ds(n * subs, subs)

    def token(t):
        return pl.ds(pl.multiple_of(t * subs, subs), subs)

    def featured(s, t, weights):
        value = weights[0] * wide[s, token(t + HEAD), :]
        for j in range(1, width):
            value = value + weights[j] * wide[s, token(t + HEAD - j), :]
        return rounded(value)

    def taps_of(s):
        return [taps_ref[at(s * width + j), :] for j in range(width)]

    decay = [jnp.exp(-rates_ref[at(n), :]) for n in range(modes)]
    taps_1, taps_2 = taps_of(1), taps_of(2)

    def first(i, carry):
        carry = list(carry)
        for u in range(UNROLL):
            t = i * UNROLL + u
            value = rounded(featured(1, t, taps_1) * featured(2, t, taps_2))
            product[token(t), :] = value
            carry = [k * m + value for k, m in zip(decay, carry)]
        return tuple(carry)

    zero = jnp.zeros((subs, LANES), jnp.float32)
    ends = lax.fori_loop(0, tokens // UNROLL, first, (zero,) * modes)
    for n in range(modes):
        total[at(n), :] = ends[n]

    def pass_on(d):
        @pl.when(z + d < nz)
        def _():
            remote(
                total, states.at[d - 1], state_send.at[d - 1], state_recv.at[d - 1],
                (lax.rem(z + d, nz), c),
            ).start()

    each(1, nz, pass_on)

    unpack(0)
    taps_0 = taps_of(0)

    def second(i, carry):
        for u in range(UNROLL):
            t = i * UNROLL + u
            query[token(t), :] = featured(0, t, taps_0)
        return carry

    lax.fori_loop(0, tokens // UNROLL, second, 0)

    def arrive(d):
        @pl.when(z >= d)
        def _():
            remote(
                total, states.at[d - 1], state_send.at[d - 1], state_recv.at[d - 1],
                (lax.rem(z + d, nz), c),
            ).wait_recv()

        @pl.when(z < d)
        def _():
            states[d - 1] = jnp.zeros((modes * subs, LANES), jnp.float32)

    each(1, nz, arrive)

    incoming = []
    for n in range(modes):
        span = jnp.exp(-rates_ref[at(n), :] * float(tokens))
        value = states[nz - 2, at(n), :]
        for d in range(nz - 2, 0, -1):
            value = value * span + states[d - 1, at(n), :]
        incoming.append(value)

    gains = [gains_ref[at(n), :] for n in range(modes)]
    skip = skip_ref[...]

    def third(i, carry):
        carry = list(carry)
        for u in range(UNROLL):
            t = i * UNROLL + u
            value = product[token(t), :]
            carry = [k * m + value for k, m in zip(decay, carry)]
            conv = added([g * m for g, m in zip(gains, carry)] + [skip * value])
            gated[token(t), :] = query[token(t), :] * conv
        return tuple(carry)

    lax.fori_loop(0, tokens // UNROLL, third, tuple(incoming))

    for j in range(parts):
        for g in range(subs):
            out_ref[j, :, g * LANES : (g + 1) * LANES] = gated[
                pl.ds(j * rows * subs + g, rows, stride=subs), :
            ].astype(jnp.bfloat16)

    @pl.when(z < nz - 1)
    def _():
        rim_copy.wait_send()

    def leave(d):
        @pl.when(z + d < nz)
        def _():
            remote(
                total, states.at[d - 1], state_send.at[d - 1], state_recv.at[d - 1],
                (lax.rem(z + d, nz), c),
            ).wait_send()

    each(1, nz, leave)


def project_kernel(
    nz, nc,
    g_ref, w_ref,
    out_ref,
    weights, stage, blocks, sent, taken, own,
    w_sem, a_send, a_recv, b_send, b_recv, s_send, s_recv, m_send, m_recv, p_send, p_recv,
):
    z, c = lax.axis_index("ctx"), lax.axis_index("ch")
    fold = nc // nz
    chips = nc // 2
    chip, core = c // 2, lax.rem(c, 2)
    mate = c + 1 - 2 * core
    tokens, columns = out_ref.shape
    rows, chans = g_ref.shape[1], g_ref.shape[2]
    tile = min(columns, 256)

    barrier = pltpu.get_barrier_semaphore()

    def greet_plane(i):
        pl.semaphore_signal(
            barrier, inc=1, device_id=(z, lax.rem(c + i, nc)), device_id_type=MESH
        )

    def greet_line(d):
        pl.semaphore_signal(
            barrier, inc=1, device_id=(lax.rem(z + d, nz), c), device_id_type=MESH
        )

    each(1, nc, greet_plane)
    each(1, nz, greet_line)
    pl.semaphore_wait(barrier, nc + nz - 2)

    w_copy = pltpu.make_async_copy(w_ref, weights, w_sem)

    def scatter(i):
        j = lax.rem(c + i, nc)
        return remote(g_ref.at[j], stage.at[c], a_send.at[i], a_recv.at[c], (z, j))

    each(1, nc, lambda i: scatter(i).start())
    own_part = pltpu.make_async_copy(g_ref.at[c], stage.at[c], a_recv.at[c])
    own_part.start()
    w_copy.start()

    edges = jnp.minimum(z, nz - 1 - z)

    def plane(s):
        paired = nz - 1 - s // 2 if s % 2 == 0 else s // 2
        single = jnp.where(2 * z < nz - 1, nz - 1 - s + edges, s - edges)
        return jnp.where(s < 2 * edges, paired, single)

    def along(s):
        q = plane(s)
        src = stage.at[pl.ds(q * fold, fold)]
        dst = blocks.at[z, :, c]
        if s == nz - 1:
            return pltpu.make_async_copy(src, dst, b_recv.at[z])
        return remote(src, dst, b_send.at[s], b_recv.at[z], (q, c))

    for s in range(nz):
        for m in range(fold):
            k = plane(s) * fold + m
            pltpu.make_async_copy(g_ref.at[0], stage.at[k], a_recv.at[k]).wait()
        along(s).start()

    def piece(k, j):
        return blocks.at[k, :, j]

    def spread(s, i):
        k = plane(s)
        to = lax.rem(chip + i, chips) * 2 + core
        return remote(piece(k, c), piece(k, c), s_send.at[s, i], s_recv.at[k, chip], (z, to))

    def hand(s, i):
        k = plane(s)
        p = lax.rem(chip + i, chips)
        j = p * 2 + core
        return remote(piece(k, j), piece(k, j), m_send.at[s, i], m_recv.at[k, p], (z, mate))

    def span(h):
        return pl.ds(h * (tokens // CHUNKS), tokens // CHUNKS)

    def back(s, h):
        k = plane(s)
        up = k > z
        to = jnp.where(up, z + 1, z - 1)
        slot = jnp.where(k == z - 1, nz, k)
        return remote(
            sent.at[s, span(h)], taken.at[slot, span(h)], p_send.at[s, h], p_recv.at[slot, h], (to, c)
        )

    def arrived(slot, h):
        there = taken.at[slot, span(h)]
        pltpu.make_async_copy(there, there, p_recv.at[slot, h]).wait()

    def over(h, body):
        each_rows = 32
        base = h * (tokens // CHUNKS)

        def go(i):
            body(pl.ds(pl.multiple_of(base + i * each_rows, each_rows), each_rows))

        pl.loop(0, tokens // CHUNKS // each_rows)(go)

    def multiply(s):
        k = plane(s)

        def strip(i):
            cols = pl.ds(pl.multiple_of(i * tile, tile), tile)
            value = jnp.zeros((tokens, tile), jnp.float32)
            for m in range(fold):
                left = blocks[k, m]
                if rows % 16:
                    left = left.astype(jnp.float32).reshape(tokens, chans).astype(jnp.bfloat16)
                else:
                    left = left.reshape(tokens, chans)
                value = value + jnp.dot(
                    left,
                    weights[m * chans : (m + 1) * chans, cols],
                    preferred_element_type=jnp.float32,
                )
            own[s, :, cols] = value

        pl.loop(0, columns // tile)(strip)

    def begin(s):
        def body(rows_at):
            sent[s, rows_at, :] = own[s, rows_at, :].astype(jnp.bfloat16)

        for h in range(CHUNKS):
            over(h, body)
            back(s, h).start()

    def relay(s):
        k = plane(s)

        def body(rows_at):
            value = own[s, rows_at, :] + taken[k, rows_at, :].astype(jnp.float32)
            sent[s, rows_at, :] = value.astype(jnp.bfloat16)

        for h in range(CHUNKS):
            arrived(k, h)
            over(h, body)
            back(s, h).start()

    for step in range(nz + 2):
        if step < nz:
            s = step
            k = plane(s)
            pltpu.make_async_copy(piece(k, c), piece(k, c), b_recv.at[k]).wait()
            each(1, chips, lambda i: spread(s, i).start())
            hand(s, 0).start()
        if 1 <= step <= nz:
            s = step - 1

            def forward(i):
                k = plane(s)
                p = lax.rem(chip + i, chips)
                remote(
                    piece(k, c), piece(k, p * 2 + core), s_send.at[s, i], s_recv.at[k, p], (z, mate)
                ).wait_recv()
                hand(s, i).start()

            each(1, chips, forward)
        if step >= 2:
            s = step - 2

            def collect(i):
                k = plane(s)
                p = lax.rem(chip + i, chips)
                remote(
                    piece(k, c), piece(k, p * 2 + 1 - core), m_send.at[s, i], m_recv.at[k, p], (z, mate)
                ).wait_recv()

            each(0, chips, collect)
            if step == 2:
                w_copy.wait()
            multiply(s)
            if s < nz - 1:
                pl.when(edges == 0)(functools.partial(begin, s))
        if 3 <= step:
            pl.when(edges > 0)(functools.partial(relay, step - 3))

    def join(slot, h):
        arrived(slot, h)

        def body(rows_at):
            own[nz - 1, rows_at, :] += taken[slot, rows_at, :].astype(jnp.float32)

        over(h, body)

    def finish(rows_at):
        out_ref[rows_at, :] = own[nz - 1, rows_at, :].astype(jnp.bfloat16)

    for h in range(CHUNKS):
        pl.when(z > 0)(functools.partial(join, z, h))
        pl.when(z < nz - 1)(functools.partial(join, nz, h))
        over(h, finish)

    each(1, nc, lambda i: scatter(i).wait_send())
    for s in range(nz - 1):
        along(s).wait_send()
        for h in range(CHUNKS):
            back(s, h).wait_send()
    for s in range(nz):
        each(1, chips, lambda i: spread(s, i).wait_send())
        each(0, chips, lambda i: hand(s, i).wait_send())


def per_device(nz, nc, features, short_weight, rates, residues, skip, out_weight):
    width = short_weight.shape[1]
    _, tokens, chans = features.shape
    modes = rates.shape[1]
    depth, columns = out_weight.shape
    subs = chans // LANES
    rows = tokens // nc
    fold = nc // nz
    chips = nc // 2
    f32, bf16 = jnp.float32, jnp.bfloat16
    vmem = pl.BlockSpec(memory_space=pltpu.VMEM)
    hbm = pl.BlockSpec(memory_space=pltpu.HBM)
    dma = pltpu.SemaphoreType.DMA

    gated = pl.pallas_call(
        functools.partial(operator_kernel, nz, modes, width),
        out_shape=jax.ShapeDtypeStruct((nc, rows, chans), bf16),
        in_specs=[hbm] + [vmem] * 4,
        out_specs=vmem,
        scratch_shapes=[
            pltpu.VMEM((3, tokens, chans), bf16),
            pltpu.VMEM((3 * width * subs, LANES), f32),
            pltpu.VMEM((modes * subs, LANES), f32),
            pltpu.VMEM((modes * subs, LANES), f32),
            pltpu.VMEM((3, RIM, chans), bf16),
            pltpu.VMEM((3, (tokens + HEAD) * subs, LANES), f32),
            pltpu.VMEM((tokens * subs, LANES), f32),
            pltpu.VMEM((tokens * subs, LANES), f32),
            pltpu.VMEM((tokens * subs, LANES), f32),
            pltpu.VMEM((modes * subs, LANES), f32),
            pltpu.VMEM((nz - 1, modes * subs, LANES), f32),
            dma((3,)), dma, dma, dma((nz - 1,)), dma((nz - 1,)),
        ],
        compiler_params=pltpu.CompilerParams(
            collective_id=0, has_side_effects=True, vmem_limit_bytes=40 * 2**20
        ),
        name="operator",
    )(
        features,
        short_weight,
        rates.T,
        residues.T,
        skip.reshape(subs, LANES),
    )

    return pl.pallas_call(
        functools.partial(project_kernel, nz, nc),
        out_shape=jax.ShapeDtypeStruct((tokens, columns), bf16),
        in_specs=[vmem, hbm],
        out_specs=vmem,
        scratch_shapes=[
            pltpu.VMEM((depth, columns), bf16),
            pltpu.VMEM((nc, rows, chans), bf16),
            pltpu.VMEM((nz, fold, nc, rows, chans), bf16),
            pltpu.VMEM((nz - 1, tokens, columns), bf16),
            pltpu.VMEM((nz + 1, tokens, columns), bf16),
            pltpu.VMEM((nz, tokens, columns), f32),
            dma,
            dma((nc,)), dma((nc,)),
            dma((nz,)), dma((nz,)),
            dma((nz, chips)), dma((nz, chips)),
            dma((nz, chips)), dma((nz, chips)),
            dma((nz - 1, CHUNKS)), dma((nz + 1, CHUNKS)),
        ],
        compiler_params=pltpu.CompilerParams(
            collective_id=1, has_side_effects=True, vmem_limit_bytes=40 * 2**20
        ),
        name="project",
    )(gated, out_weight)


def solution(mesh):
    return jax.shard_map(
        functools.partial(per_device, mesh.shape["ctx"], mesh.shape["ch"]),
        mesh=mesh,
        in_specs=(
            P(None, "ctx", "ch"),
            P(None, None, "ch"),
            P("ch", None),
            P("ch", None),
            P("ch"),
            P("ctx", "ch"),
        ),
        out_specs=P("ctx", "ch"),
        check_vma=False,
    )
```

```python
import functools
import jax
import jax.numpy as jnp
from jax import lax
from jax.experimental import pallas as pl
from jax.experimental.pallas import tpu as pltpu
from jax.sharding import PartitionSpec as P

MESH = pl.DeviceIdType.MESH
LANES = 128
HEAD = 8
RIM = 16
UNROLL = 8
CHUNKS = 2


def each(low, high, body):
    if high - low <= 8:
        for i in range(low, high):
            body(i)
    else:

        def step(i, carry):
            body(i)
            return carry

        lax.fori_loop(low, high, step, 0)


def remote(src, dst, send_sem, recv_sem, device):
    return pltpu.make_async_remote_copy(
        src_ref=src,
        dst_ref=dst,
        send_sem=send_sem,
        recv_sem=recv_sem,
        device_id=device,
        device_id_type=MESH,
    )


def rounded(value):
    return value.astype(jnp.bfloat16).astype(jnp.float32)


def added(terms):
    while len(terms) > 1:
        terms = [a + b for a, b in zip(terms[::2], terms[1::2])] + (
            [terms[-1]] if len(terms) % 2 else []
        )
    return terms[0]


def operator_kernel(
    nz, nc, modes, width,
    feat_hbm, taps_hbm, rates_hbm, gains_hbm, skip_hbm, w_ref,
    out_ref,
    feat_ref, taps_in, rates_in, gains_in, skip_ref, taps_ref, rates_ref, gains_ref,
    rim, wide, product, query, gated, total, states,
    g_ref, weights, stage, blocks, sent, taken, own,
    feat_sem, rim_send, rim_recv, state_send, state_recv, small_sem,
    w_sem, a_send, a_recv, b_send, b_recv, s_send, s_recv, m_send, m_recv, p_send, p_recv,
):
    z, c = lax.axis_index("ctx"), lax.axis_index("ch")
    tokens, chans = feat_hbm.shape[1], feat_hbm.shape[2]
    subs = chans // LANES
    rows = g_ref.shape[1]
    columns = out_ref.shape[1]
    fold = nc // nz
    chips = nc // 2
    chip, core = c // 2, lax.rem(c, 2)
    mate = c + 1 - 2 * core
    tile = min(columns, 256)

    def load(s):
        return pltpu.make_async_copy(feat_hbm.at[s], feat_ref.at[s], feat_sem.at[s])

    small = [
        pltpu.make_async_copy(src, dst, small_sem.at[i])
        for i, (src, dst) in enumerate(
            ((taps_hbm, taps_in), (rates_hbm, rates_in), (gains_hbm, gains_in), (skip_hbm, skip_ref))
        )
    ]
    w_copy = pltpu.make_async_copy(w_ref, weights, w_sem)

    barrier = pltpu.get_barrier_semaphore()

    def greet_line(d):
        pl.semaphore_signal(
            barrier, inc=1, device_id=(lax.rem(z + d, nz), c), device_id_type=MESH
        )

    def greet_plane(i):
        pl.semaphore_signal(
            barrier, inc=1, device_id=(z, lax.rem(c + i, nc)), device_id_type=MESH
        )

    each(1, nz, greet_line)
    each(1, nc, greet_plane)
    for copy in small:
        copy.start()
    for s in (1, 2, 0):
        load(s).start()
    w_copy.start()
    for copy in small:
        copy.wait()

    for g in range(subs):
        lanes = slice(g * LANES, (g + 1) * LANES)
        rates_ref[pl.ds(g, modes, stride=subs), :] = rates_in[:, lanes]
        gains_ref[pl.ds(g, modes, stride=subs), :] = gains_in[:, lanes]
        for s in range(3):
            taps_ref[pl.ds(s * width * subs + g, width, stride=subs), :] = taps_in[s, :, lanes]

    pl.semaphore_wait(barrier, nc + nz - 2)

    rim_copy = remote(
        feat_hbm.at[:, pl.ds(tokens - RIM, RIM), :], rim, rim_send, rim_recv,
        (lax.rem(z + 1, nz), c),
    )

    @pl.when(z < nz - 1)
    def _():
        rim_copy.start()

    def unpack(s):
        load(s).wait()
        for g in range(subs):
            wide[s, pl.ds(HEAD * subs + g, tokens, stride=subs), :] = feat_ref[
                s, :, g * LANES : (g + 1) * LANES
            ].astype(jnp.float32)

    unpack(1)
    unpack(2)

    @pl.when(z > 0)
    def _():
        rim_copy.wait_recv()
        for s in range(3):
            for g in range(subs):
                part = rim[s, :, g * LANES : (g + 1) * LANES].astype(jnp.float32)
                wide[s, pl.ds(g, HEAD, stride=subs), :] = part[RIM - HEAD :, :]

    @pl.when(z == 0)
    def _():
        wide[:, pl.ds(0, HEAD * subs), :] = jnp.zeros((3, HEAD * subs, LANES), jnp.float32)

    def at(n):
        return pl.ds(n * subs, subs)

    def token(t):
        return pl.ds(pl.multiple_of(t * subs, subs), subs)

    def featured(s, t, weights):
        value = weights[0] * wide[s, token(t + HEAD), :]
        for j in range(1, width):
            value = value + weights[j] * wide[s, token(t + HEAD - j), :]
        return rounded(value)

    def taps_of(s):
        return [taps_ref[at(s * width + j), :] for j in range(width)]

    decay = [jnp.exp(-rates_ref[at(n), :]) for n in range(modes)]
    taps_1, taps_2 = taps_of(1), taps_of(2)

    def first(i, carry):
        carry = list(carry)
        for u in range(UNROLL):
            t = i * UNROLL + u
            value = rounded(featured(1, t, taps_1) * featured(2, t, taps_2))
            product[token(t), :] = value
            carry = [k * m + value for k, m in zip(decay, carry)]
        return tuple(carry)

    zero = jnp.zeros((subs, LANES), jnp.float32)
    ends = lax.fori_loop(0, tokens // UNROLL, first, (zero,) * modes)
    for n in range(modes):
        total[at(n), :] = ends[n]

    def pass_on(d):
        @pl.when(z + d < nz)
        def _():
            remote(
                total, states.at[d - 1], state_send.at[d - 1], state_recv.at[d - 1],
                (lax.rem(z + d, nz), c),
            ).start()

    each(1, nz, pass_on)

    unpack(0)
    taps_0 = taps_of(0)

    def second(i, carry):
        for u in range(UNROLL):
            t = i * UNROLL + u
            query[token(t), :] = featured(0, t, taps_0)
        return carry

    lax.fori_loop(0, tokens // UNROLL, second, 0)

    def arrive(d):
        @pl.when(z >= d)
        def _():
            remote(
                total, states.at[d - 1], state_send.at[d - 1], state_recv.at[d - 1],
                (lax.rem(z + d, nz), c),
            ).wait_recv()

        @pl.when(z < d)
        def _():
            states[d - 1] = jnp.zeros((modes * subs, LANES), jnp.float32)

    each(1, nz, arrive)

    incoming = []
    for n in range(modes):
        span = jnp.exp(-rates_ref[at(n), :] * float(tokens))
        value = states[nz - 2, at(n), :]
        for d in range(nz - 2, 0, -1):
            value = value * span + states[d - 1, at(n), :]
        incoming.append(value)

    gains = [gains_ref[at(n), :] for n in range(modes)]
    skip = skip_ref[...]

    def scatter(j):
        return remote(g_ref.at[j], stage.at[c], a_send.at[j], a_recv.at[c], (z, j))

    def portion(j, carry):
        def third(i, carry):
            carry = list(carry)
            for u in range(UNROLL):
                t = j * rows + i * UNROLL + u
                value = product[token(t), :]
                carry = [k * m + value for k, m in zip(decay, carry)]
                conv = added([g * m for g, m in zip(gains, carry)] + [skip * value])
                gated[token(i * UNROLL + u), :] = query[token(t), :] * conv
            return tuple(carry)

        carry = lax.fori_loop(0, rows // UNROLL, third, carry)
        for g in range(subs):
            g_ref[j, :, g * LANES : (g + 1) * LANES] = gated[
                pl.ds(g, rows, stride=subs), :
            ].astype(jnp.bfloat16)

        @pl.when(j != c)
        def _():
            scatter(j).start()

        @pl.when(j == c)
        def _():
            pltpu.make_async_copy(g_ref.at[c], stage.at[c], a_recv.at[c]).start()

        return carry

    lax.fori_loop(0, nc, portion, tuple(incoming))

    edges = jnp.minimum(z, nz - 1 - z)

    def plane(s):
        paired = nz - 1 - s // 2 if s % 2 == 0 else s // 2
        single = jnp.where(2 * z < nz - 1, nz - 1 - s + edges, s - edges)
        return jnp.where(s < 2 * edges, paired, single)

    def along(s):
        q = plane(s)
        src = stage.at[pl.ds(q * fold, fold)]
        dst = blocks.at[z, :, c]
        if s == nz - 1:
            return pltpu.make_async_copy(src, dst, b_recv.at[z])
        return remote(src, dst, b_send.at[s], b_recv.at[z], (q, c))

    def send_along():
        for s in range(nz):
            for m in range(fold):
                k = plane(s) * fold + m
                pltpu.make_async_copy(g_ref.at[0], stage.at[k], a_recv.at[k]).wait()
            along(s).start()

    def piece(k, j):
        return blocks.at[k, :, j]

    def spread(s, i):
        k = plane(s)
        to = lax.rem(chip + i, chips) * 2 + core
        return remote(piece(k, c), piece(k, c), s_send.at[s, i], s_recv.at[k, chip], (z, to))

    def hand(s, i):
        k = plane(s)
        p = lax.rem(chip + i, chips)
        j = p * 2 + core
        return remote(piece(k, j), piece(k, j), m_send.at[s, i], m_recv.at[k, p], (z, mate))

    def span(h):
        return pl.ds(h * (tokens // CHUNKS), tokens // CHUNKS)

    def back(s, h):
        k = plane(s)
        up = k > z
        to = jnp.where(up, z + 1, z - 1)
        slot = jnp.where(k == z - 1, nz, k)
        return remote(
            sent.at[s, span(h)], taken.at[slot, span(h)], p_send.at[s, h], p_recv.at[slot, h], (to, c)
        )

    def arrived(slot, h):
        there = taken.at[slot, span(h)]
        pltpu.make_async_copy(there, there, p_recv.at[slot, h]).wait()

    def over(h, body):
        each_rows = 32
        base = h * (tokens // CHUNKS)

        def go(i):
            body(pl.ds(pl.multiple_of(base + i * each_rows, each_rows), each_rows))

        pl.loop(0, tokens // CHUNKS // each_rows)(go)

    def multiply(s):
        k = plane(s)

        def strip(i):
            cols = pl.ds(pl.multiple_of(i * tile, tile), tile)
            value = jnp.zeros((tokens, tile), jnp.float32)
            for m in range(fold):
                left = blocks[k, m]
                if rows % 16:
                    left = left.astype(jnp.float32).reshape(tokens, chans).astype(jnp.bfloat16)
                else:
                    left = left.reshape(tokens, chans)
                value = value + jnp.dot(
                    left,
                    weights[m * chans : (m + 1) * chans, cols],
                    preferred_element_type=jnp.float32,
                )
            own[s, :, cols] = value

        pl.loop(0, columns // tile)(strip)

    def begin(s):
        def body(rows_at):
            sent[s, rows_at, :] = own[s, rows_at, :].astype(jnp.bfloat16)

        for h in range(CHUNKS):
            over(h, body)
            back(s, h).start()

    def relay(s):
        k = plane(s)

        def body(rows_at):
            value = own[s, rows_at, :] + taken[k, rows_at, :].astype(jnp.float32)
            sent[s, rows_at, :] = value.astype(jnp.bfloat16)

        for h in range(CHUNKS):
            arrived(k, h)
            over(h, body)
            back(s, h).start()

    def begin_block(s):
        k = plane(s)
        pltpu.make_async_copy(piece(k, c), piece(k, c), b_recv.at[k]).wait()
        each(1, chips, lambda i: spread(s, i).start())
        hand(s, 0).start()

    def forward_block(s):
        k = plane(s)

        def forward(i):
            p = lax.rem(chip + i, chips)
            remote(
                piece(k, c), piece(k, p * 2 + core), s_send.at[s, i], s_recv.at[k, p], (z, mate)
            ).wait_recv()
            hand(s, i).start()

        each(1, chips, forward)

    def collect_block(s):
        k = plane(s)

        def collect(i):
            p = lax.rem(chip + i, chips)
            remote(
                piece(k, c), piece(k, p * 2 + 1 - core), m_send.at[s, i], m_recv.at[k, p], (z, mate)
            ).wait_recv()

        each(0, chips, collect)

    pl.when(edges == 0)(send_along)
    begin_block(0)
    pl.when(edges > 0)(send_along)
    for s in range(nz):
        forward_block(s)
        if s < nz - 1:
            begin_block(s + 1)
        collect_block(s)
        if s == 0:
            w_copy.wait()
        multiply(s)
        if s < nz - 1:
            pl.when(edges == 0)(functools.partial(begin, s))
        if s > 0:
            pl.when(edges > 0)(functools.partial(relay, s - 1))

    def join(slot, h):
        arrived(slot, h)

        def body(rows_at):
            own[nz - 1, rows_at, :] += taken[slot, rows_at, :].astype(jnp.float32)

        over(h, body)

    def finish(rows_at):
        out_ref[rows_at, :] = own[nz - 1, rows_at, :].astype(jnp.bfloat16)

    for h in range(CHUNKS):
        pl.when(z > 0)(functools.partial(join, z, h))
        pl.when(z < nz - 1)(functools.partial(join, nz, h))
        over(h, finish)

    @pl.when(z < nz - 1)
    def _():
        rim_copy.wait_send()

    def leave(d):
        @pl.when(z + d < nz)
        def _():
            remote(
                total, states.at[d - 1], state_send.at[d - 1], state_recv.at[d - 1],
                (lax.rem(z + d, nz), c),
            ).wait_send()

    each(1, nz, leave)
    each(1, nc, lambda i: scatter(lax.rem(c + i, nc)).wait_send())
    for s in range(nz - 1):
        along(s).wait_send()
        for h in range(CHUNKS):
            back(s, h).wait_send()
    for s in range(nz):
        each(1, chips, lambda i: spread(s, i).wait_send())
        each(0, chips, lambda i: hand(s, i).wait_send())


def per_device(nz, nc, features, short_weight, rates, residues, skip, out_weight):
    width = short_weight.shape[1]
    _, tokens, chans = features.shape
    modes = rates.shape[1]
    depth, columns = out_weight.shape
    subs = chans // LANES
    rows = tokens // nc
    fold = nc // nz
    chips = nc // 2
    f32, bf16 = jnp.float32, jnp.bfloat16
    vmem = pl.BlockSpec(memory_space=pltpu.VMEM)
    hbm = pl.BlockSpec(memory_space=pltpu.HBM)
    dma = pltpu.SemaphoreType.DMA

    return pl.pallas_call(
        functools.partial(operator_kernel, nz, nc, modes, width),
        out_shape=jax.ShapeDtypeStruct((tokens, columns), bf16),
        in_specs=[hbm] * 6,
        out_specs=vmem,
        scratch_shapes=[
            pltpu.VMEM((3, tokens, chans), bf16),
            pltpu.VMEM((3, width, chans), f32),
            pltpu.VMEM((modes, chans), f32),
            pltpu.VMEM((modes, chans), f32),
            pltpu.VMEM((subs, LANES), f32),
            pltpu.VMEM((3 * width * subs, LANES), f32),
            pltpu.VMEM((modes * subs, LANES), f32),
            pltpu.VMEM((modes * subs, LANES), f32),
            pltpu.VMEM((3, RIM, chans), bf16),
            pltpu.VMEM((3, (tokens + HEAD) * subs, LANES), f32),
            pltpu.VMEM((tokens * subs, LANES), f32),
            pltpu.VMEM((tokens * subs, LANES), f32),
            pltpu.VMEM((rows * subs, LANES), f32),
            pltpu.VMEM((modes * subs, LANES), f32),
            pltpu.VMEM((nz - 1, modes * subs, LANES), f32),
            pltpu.VMEM((nc, rows, chans), bf16),
            pltpu.VMEM((depth, columns), bf16),
            pltpu.VMEM((nc, rows, chans), bf16),
            pltpu.VMEM((nz, fold, nc, rows, chans), bf16),
            pltpu.VMEM((nz - 1, tokens, columns), bf16),
            pltpu.VMEM((nz + 1, tokens, columns), bf16),
            pltpu.VMEM((nz, tokens, columns), f32),
            dma((3,)), dma, dma, dma((nz - 1,)), dma((nz - 1,)), dma((4,)),
            dma,
            dma((nc,)), dma((nc,)),
            dma((nz,)), dma((nz,)),
            dma((nz, chips)), dma((nz, chips)),
            dma((nz, chips)), dma((nz, chips)),
            dma((nz - 1, CHUNKS)), dma((nz + 1, CHUNKS)),
        ],
        compiler_params=pltpu.CompilerParams(
            collective_id=0, has_side_effects=True, vmem_limit_bytes=62 * 2**20
        ),
        name="operator",
    )(features, short_weight, rates.T, residues.T, skip.reshape(subs, LANES), out_weight)


def solution(mesh):
    return jax.shard_map(
        functools.partial(per_device, mesh.shape["ctx"], mesh.shape["ch"]),
        mesh=mesh,
        in_specs=(
            P(None, "ctx", "ch"),
            P(None, None, "ch"),
            P("ch", None),
            P("ch", None),
            P("ch"),
            P("ctx", "ch"),
        ),
        out_specs=P("ctx", "ch"),
        check_vma=False,
    )
```

```python
import functools
import jax
import jax.numpy as jnp
from jax import lax
from jax.experimental import pallas as pl
from jax.experimental.pallas import tpu as pltpu
from jax.sharding import PartitionSpec as P

MESH = pl.DeviceIdType.MESH
LANES = 128
HEAD = 8
RIM = 16
UNROLL = 8
CHUNKS = 2


def each(low, high, body):
    if high - low <= 8:
        for i in range(low, high):
            body(i)
    else:

        def step(i, carry):
            body(i)
            return carry

        lax.fori_loop(low, high, step, 0)


def remote(src, dst, send_sem, recv_sem, device):
    return pltpu.make_async_remote_copy(
        src_ref=src,
        dst_ref=dst,
        send_sem=send_sem,
        recv_sem=recv_sem,
        device_id=device,
        device_id_type=MESH,
    )


def rounded(value):
    return value.astype(jnp.bfloat16).astype(jnp.float32)


def added(terms):
    while len(terms) > 1:
        terms = [a + b for a, b in zip(terms[::2], terms[1::2])] + (
            [terms[-1]] if len(terms) % 2 else []
        )
    return terms[0]


def operator_kernel(
    nz, nc, modes, width,
    feat_hbm, taps_hbm, rates_hbm, gains_hbm, skip_hbm, w_ref,
    out_ref,
    feat_ref, taps_in, rates_in, gains_in, skip_ref, taps_ref, rates_ref, gains_ref,
    rim, wide, product, query, gated, total, states,
    g_ref, weights, stage, blocks, sent, taken, own,
    feat_sem, rim_send, rim_recv, state_send, state_recv, small_sem,
    w_sem, a_send, a_recv, b_send, b_recv, s_send, s_recv, m_send, m_recv, p_send, p_recv,
):
    z, c = lax.axis_index("ctx"), lax.axis_index("ch")
    tokens, chans = feat_hbm.shape[1], feat_hbm.shape[2]
    subs = chans // LANES
    rows = g_ref.shape[1]
    columns = out_ref.shape[1]
    fold = nc // nz
    chips = nc // 2
    chip, core = c // 2, lax.rem(c, 2)
    mate = c + 1 - 2 * core
    tile = min(columns, 256)

    def load(s):
        return pltpu.make_async_copy(feat_hbm.at[s], feat_ref.at[s], feat_sem.at[s])

    small = [
        pltpu.make_async_copy(src, dst, small_sem.at[i])
        for i, (src, dst) in enumerate(
            ((taps_hbm, taps_in), (rates_hbm, rates_in), (gains_hbm, gains_in), (skip_hbm, skip_ref))
        )
    ]
    w_copy = pltpu.make_async_copy(w_ref, weights, w_sem)

    barrier = pltpu.get_barrier_semaphore()

    def greet_line(d):
        pl.semaphore_signal(
            barrier, inc=1, device_id=(lax.rem(z + d, nz), c), device_id_type=MESH
        )

    def greet_plane(i):
        pl.semaphore_signal(
            barrier, inc=1, device_id=(z, lax.rem(c + i, nc)), device_id_type=MESH
        )

    each(1, nz, greet_line)
    each(1, nc, greet_plane)
    for copy in small:
        copy.start()
    for s in (1, 2, 0):
        load(s).start()
    w_copy.start()
    for copy in small:
        copy.wait()

    for g in range(subs):
        lanes = slice(g * LANES, (g + 1) * LANES)
        rates_ref[pl.ds(g, modes, stride=subs), :] = rates_in[:, lanes]
        gains_ref[pl.ds(g, modes, stride=subs), :] = gains_in[:, lanes]
        for s in range(3):
            taps_ref[pl.ds(s * width * subs + g, width, stride=subs), :] = taps_in[s, :, lanes]

    pl.semaphore_wait(barrier, nc + nz - 2)

    rim_copy = remote(
        feat_hbm.at[:, pl.ds(tokens - RIM, RIM), :], rim, rim_send, rim_recv,
        (lax.rem(z + 1, nz), c),
    )

    @pl.when(z < nz - 1)
    def _():
        rim_copy.start()

    def unpack(s):
        load(s).wait()
        for g in range(subs):
            wide[s, pl.ds(HEAD * subs + g, tokens, stride=subs), :] = feat_ref[
                s, :, g * LANES : (g + 1) * LANES
            ].astype(jnp.float32)

    unpack(1)
    unpack(2)

    @pl.when(z > 0)
    def _():
        rim_copy.wait_recv()
        for s in range(3):
            for g in range(subs):
                part = rim[s, :, g * LANES : (g + 1) * LANES].astype(jnp.float32)
                wide[s, pl.ds(g, HEAD, stride=subs), :] = part[RIM - HEAD :, :]

    @pl.when(z == 0)
    def _():
        wide[:, pl.ds(0, HEAD * subs), :] = jnp.zeros((3, HEAD * subs, LANES), jnp.float32)

    def at(n):
        return pl.ds(n * subs, subs)

    def token(t):
        return pl.ds(pl.multiple_of(t * subs, subs), subs)

    def featured(s, t, weights):
        value = weights[0] * wide[s, token(t + HEAD), :]
        for j in range(1, width):
            value = value + weights[j] * wide[s, token(t + HEAD - j), :]
        return rounded(value)

    def taps_of(s):
        return [taps_ref[at(s * width + j), :] for j in range(width)]

    decay = [jnp.exp(-rates_ref[at(n), :]) for n in range(modes)]
    taps_1, taps_2 = taps_of(1), taps_of(2)

    def first(i, carry):
        carry = list(carry)
        for u in range(UNROLL):
            t = i * UNROLL + u
            value = rounded(featured(1, t, taps_1) * featured(2, t, taps_2))
            product[token(t), :] = value
            carry = [k * m + value for k, m in zip(decay, carry)]
        return tuple(carry)

    zero = jnp.zeros((subs, LANES), jnp.float32)
    ends = lax.fori_loop(0, tokens // UNROLL, first, (zero,) * modes)
    for n in range(modes):
        total[at(n), :] = ends[n]

    def pass_on(d):
        @pl.when(z + d < nz)
        def _():
            remote(
                total, states.at[d - 1], state_send.at[d - 1], state_recv.at[d - 1],
                (lax.rem(z + d, nz), c),
            ).start()

    each(1, nz, pass_on)

    unpack(0)
    taps_0 = taps_of(0)

    def second(i, carry):
        for u in range(UNROLL):
            t = i * UNROLL + u
            query[token(t), :] = featured(0, t, taps_0)
        return carry

    lax.fori_loop(0, tokens // UNROLL, second, 0)

    def arrive(d):
        @pl.when(z >= d)
        def _():
            remote(
                total, states.at[d - 1], state_send.at[d - 1], state_recv.at[d - 1],
                (lax.rem(z + d, nz), c),
            ).wait_recv()

        @pl.when(z < d)
        def _():
            states[d - 1] = jnp.zeros((modes * subs, LANES), jnp.float32)

    each(1, nz, arrive)

    incoming = []
    for n in range(modes):
        span = jnp.exp(-rates_ref[at(n), :] * float(tokens))
        value = states[nz - 2, at(n), :]
        for d in range(nz - 2, 0, -1):
            value = value * span + states[d - 1, at(n), :]
        incoming.append(value)

    gains = [gains_ref[at(n), :] for n in range(modes)]
    skip = skip_ref[...]

    def scatter(j):
        return remote(g_ref.at[j], stage.at[c], a_send.at[j], a_recv.at[c], (z, j))

    def portion(j, carry):
        def third(i, carry):
            carry = list(carry)
            for u in range(UNROLL):
                t = j * rows + i * UNROLL + u
                value = product[token(t), :]
                carry = [k * m + value for k, m in zip(decay, carry)]
                conv = added([g * m for g, m in zip(gains, carry)] + [skip * value])
                gated[token(i * UNROLL + u), :] = query[token(t), :] * conv
            return tuple(carry)

        carry = lax.fori_loop(0, rows // UNROLL, third, carry)
        for g in range(subs):
            g_ref[j, :, g * LANES : (g + 1) * LANES] = gated[
                pl.ds(g, rows, stride=subs), :
            ].astype(jnp.bfloat16)

        @pl.when(j != c)
        def _():
            scatter(j).start()

        @pl.when(j == c)
        def _():
            pltpu.make_async_copy(g_ref.at[c], stage.at[c], a_recv.at[c]).start()

        return carry

    lax.fori_loop(0, nc, portion, tuple(incoming))

    edges = jnp.minimum(z, nz - 1 - z)

    def plane(s):
        far = (nz - 1 - s // 2, s // 2)
        paired = jnp.where(2 * z < nz - 1, far[s % 2], far[1 - s % 2])
        single = jnp.where(2 * z < nz - 1, nz - 1 - s + edges, s - edges)
        return jnp.where(s < 2 * edges, paired, single)

    def along(s):
        q = plane(s)
        src = stage.at[pl.ds(q * fold, fold)]
        dst = blocks.at[z, :, c]
        if s == nz - 1:
            return pltpu.make_async_copy(src, dst, b_recv.at[z])
        return remote(src, dst, b_send.at[s], b_recv.at[z], (q, c))

    def send_along():
        for s in range(nz):
            for m in range(fold):
                k = plane(s) * fold + m
                pltpu.make_async_copy(g_ref.at[0], stage.at[k], a_recv.at[k]).wait()
            along(s).start()

    def piece(k, j):
        return blocks.at[k, :, j]

    def spread(s, i):
        k = plane(s)
        to = lax.rem(chip + i, chips) * 2 + core
        return remote(piece(k, c), piece(k, c), s_send.at[s, i], s_recv.at[k, chip], (z, to))

    def hand(s, i):
        k = plane(s)
        p = lax.rem(chip + i, chips)
        j = p * 2 + core
        return remote(piece(k, j), piece(k, j), m_send.at[s, i], m_recv.at[k, p], (z, mate))

    def span(h):
        return pl.ds(h * (tokens // CHUNKS), tokens // CHUNKS)

    def back(s, h):
        k = plane(s)
        up = k > z
        to = jnp.where(up, z + 1, z - 1)
        slot = jnp.where(k == z - 1, nz, k)
        return remote(
            sent.at[s, span(h)], taken.at[slot, span(h)], p_send.at[s, h], p_recv.at[slot, h], (to, c)
        )

    def arrived(slot, h):
        there = taken.at[slot, span(h)]
        pltpu.make_async_copy(there, there, p_recv.at[slot, h]).wait()

    def over(h, body):
        each_rows = 32
        base = h * (tokens // CHUNKS)

        def go(i):
            body(pl.ds(pl.multiple_of(base + i * each_rows, each_rows), each_rows))

        pl.loop(0, tokens // CHUNKS // each_rows)(go)

    def multiply(s):
        k = plane(s)

        def strip(i):
            cols = pl.ds(pl.multiple_of(i * tile, tile), tile)
            value = jnp.zeros((tokens, tile), jnp.float32)
            for m in range(fold):
                left = blocks[k, m]
                if rows % 16:
                    left = left.astype(jnp.float32).reshape(tokens, chans).astype(jnp.bfloat16)
                else:
                    left = left.reshape(tokens, chans)
                value = value + jnp.dot(
                    left,
                    weights[m * chans : (m + 1) * chans, cols],
                    preferred_element_type=jnp.float32,
                )
            own[s, :, cols] = value

        pl.loop(0, columns // tile)(strip)

    def begin(s):
        def body(rows_at):
            sent[s, rows_at, :] = own[s, rows_at, :].astype(jnp.bfloat16)

        for h in range(CHUNKS):
            over(h, body)
            back(s, h).start()

    def relay(s):
        k = plane(s)

        def body(rows_at):
            value = own[s, rows_at, :] + taken[k, rows_at, :].astype(jnp.float32)
            sent[s, rows_at, :] = value.astype(jnp.bfloat16)

        for h in range(CHUNKS):
            arrived(k, h)
            over(h, body)
            back(s, h).start()

    def begin_block(s):
        k = plane(s)
        pltpu.make_async_copy(piece(k, c), piece(k, c), b_recv.at[k]).wait()
        each(1, chips, lambda i: spread(s, i).start())
        hand(s, 0).start()

    def forward_block(s):
        k = plane(s)

        def forward(i):
            p = lax.rem(chip + i, chips)
            remote(
                piece(k, c), piece(k, p * 2 + core), s_send.at[s, i], s_recv.at[k, p], (z, mate)
            ).wait_recv()
            hand(s, i).start()

        each(1, chips, forward)

    def collect_block(s):
        k = plane(s)

        def collect(i):
            p = lax.rem(chip + i, chips)
            remote(
                piece(k, c), piece(k, p * 2 + 1 - core), m_send.at[s, i], m_recv.at[k, p], (z, mate)
            ).wait_recv()

        each(0, chips, collect)

    pl.when(edges == 0)(send_along)
    begin_block(0)
    pl.when(edges > 0)(send_along)
    for s in range(nz):
        forward_block(s)
        if s < nz - 1:
            begin_block(s + 1)
        collect_block(s)
        if s == 0:
            w_copy.wait()
        multiply(s)
        if s < nz - 1:
            pl.when(edges == 0)(functools.partial(begin, s))
        if s > 0:
            pl.when(edges > 0)(functools.partial(relay, s - 1))

    def join(slot, h):
        arrived(slot, h)

        def body(rows_at):
            own[nz - 1, rows_at, :] += taken[slot, rows_at, :].astype(jnp.float32)

        over(h, body)

    def finish(rows_at):
        out_ref[rows_at, :] = own[nz - 1, rows_at, :].astype(jnp.bfloat16)

    for h in range(CHUNKS):
        pl.when(z > 0)(functools.partial(join, z, h))
        pl.when(z < nz - 1)(functools.partial(join, nz, h))
        over(h, finish)

    @pl.when(z < nz - 1)
    def _():
        rim_copy.wait_send()

    def leave(d):
        @pl.when(z + d < nz)
        def _():
            remote(
                total, states.at[d - 1], state_send.at[d - 1], state_recv.at[d - 1],
                (lax.rem(z + d, nz), c),
            ).wait_send()

    each(1, nz, leave)
    each(1, nc, lambda i: scatter(lax.rem(c + i, nc)).wait_send())
    for s in range(nz - 1):
        along(s).wait_send()
        for h in range(CHUNKS):
            back(s, h).wait_send()
    for s in range(nz):
        each(1, chips, lambda i: spread(s, i).wait_send())
        each(0, chips, lambda i: hand(s, i).wait_send())


def per_device(nz, nc, features, short_weight, rates, residues, skip, out_weight):
    width = short_weight.shape[1]
    _, tokens, chans = features.shape
    modes = rates.shape[1]
    depth, columns = out_weight.shape
    subs = chans // LANES
    rows = tokens // nc
    fold = nc // nz
    chips = nc // 2
    f32, bf16 = jnp.float32, jnp.bfloat16
    vmem = pl.BlockSpec(memory_space=pltpu.VMEM)
    hbm = pl.BlockSpec(memory_space=pltpu.HBM)
    dma = pltpu.SemaphoreType.DMA

    return pl.pallas_call(
        functools.partial(operator_kernel, nz, nc, modes, width),
        out_shape=jax.ShapeDtypeStruct((tokens, columns), bf16),
        in_specs=[hbm] * 6,
        out_specs=vmem,
        scratch_shapes=[
            pltpu.VMEM((3, tokens, chans), bf16),
            pltpu.VMEM((3, width, chans), f32),
            pltpu.VMEM((modes, chans), f32),
            pltpu.VMEM((modes, chans), f32),
            pltpu.VMEM((subs, LANES), f32),
            pltpu.VMEM((3 * width * subs, LANES), f32),
            pltpu.VMEM((modes * subs, LANES), f32),
            pltpu.VMEM((modes * subs, LANES), f32),
            pltpu.VMEM((3, RIM, chans), bf16),
            pltpu.VMEM((3, (tokens + HEAD) * subs, LANES), f32),
            pltpu.VMEM((tokens * subs, LANES), f32),
            pltpu.VMEM((tokens * subs, LANES), f32),
            pltpu.VMEM((rows * subs, LANES), f32),
            pltpu.VMEM((modes * subs, LANES), f32),
            pltpu.VMEM((nz - 1, modes * subs, LANES), f32),
            pltpu.VMEM((nc, rows, chans), bf16),
            pltpu.VMEM((depth, columns), bf16),
            pltpu.VMEM((nc, rows, chans), bf16),
            pltpu.VMEM((nz, fold, nc, rows, chans), bf16),
            pltpu.VMEM((nz - 1, tokens, columns), bf16),
            pltpu.VMEM((nz + 1, tokens, columns), bf16),
            pltpu.VMEM((nz, tokens, columns), f32),
            dma((3,)), dma, dma, dma((nz - 1,)), dma((nz - 1,)), dma((4,)),
            dma,
            dma((nc,)), dma((nc,)),
            dma((nz,)), dma((nz,)),
            dma((nz, chips)), dma((nz, chips)),
            dma((nz, chips)), dma((nz, chips)),
            dma((nz - 1, CHUNKS)), dma((nz + 1, CHUNKS)),
        ],
        compiler_params=pltpu.CompilerParams(
            collective_id=0, has_side_effects=True, vmem_limit_bytes=62 * 2**20
        ),
        name="operator",
    )(features, short_weight, rates.T, residues.T, skip.reshape(subs, LANES), out_weight)


def solution(mesh):
    return jax.shard_map(
        functools.partial(per_device, mesh.shape["ctx"], mesh.shape["ch"]),
        mesh=mesh,
        in_specs=(
            P(None, "ctx", "ch"),
            P(None, None, "ch"),
            P("ch", None),
            P("ch", None),
            P("ch"),
            P("ctx", "ch"),
        ),
        out_specs=P("ctx", "ch"),
        check_vma=False,
    )
```

```python
import functools
import jax
import jax.numpy as jnp
from jax import lax
from jax.experimental import pallas as pl
from jax.experimental.pallas import tpu as pltpu
from jax.sharding import PartitionSpec as P

MESH = pl.DeviceIdType.MESH
LANES = 128
HEAD = 8
RIM = 16
UNROLL = 8
CHUNKS = 4


def each(low, high, body):
    if high - low <= 8:
        for i in range(low, high):
            body(i)
    else:

        def step(i, carry):
            body(i)
            return carry

        lax.fori_loop(low, high, step, 0)


def remote(src, dst, send_sem, recv_sem, device):
    return pltpu.make_async_remote_copy(
        src_ref=src,
        dst_ref=dst,
        send_sem=send_sem,
        recv_sem=recv_sem,
        device_id=device,
        device_id_type=MESH,
    )


def rounded(value):
    return value.astype(jnp.bfloat16).astype(jnp.float32)


def added(terms):
    while len(terms) > 1:
        terms = [a + b for a, b in zip(terms[::2], terms[1::2])] + (
            [terms[-1]] if len(terms) % 2 else []
        )
    return terms[0]


def operator_kernel(
    nz, nc, modes, width,
    feat_hbm, taps_hbm, rates_hbm, gains_hbm, skip_hbm, w_ref,
    out_ref,
    feat_ref, taps_in, rates_in, gains_in, skip_ref, taps_ref, rates_ref, gains_ref,
    rim, wide, product, query, gated, total, states,
    g_ref, weights, stage, blocks, sent, taken, own,
    feat_sem, rim_send, rim_recv, state_send, state_recv, small_sem,
    w_sem, a_send, a_recv, b_send, b_recv, s_send, s_recv, m_send, m_recv, p_send, p_recv,
):
    z, c = lax.axis_index("ctx"), lax.axis_index("ch")
    tokens, chans = feat_hbm.shape[1], feat_hbm.shape[2]
    subs = chans // LANES
    rows = g_ref.shape[1]
    columns = out_ref.shape[1]
    fold = nc // nz
    chips = nc // 2
    chip, core = c // 2, lax.rem(c, 2)
    mate = c + 1 - 2 * core
    tile = min(columns, 256)

    def load(s):
        return pltpu.make_async_copy(feat_hbm.at[s], feat_ref.at[s], feat_sem.at[s])

    small = [
        pltpu.make_async_copy(src, dst, small_sem.at[i])
        for i, (src, dst) in enumerate(
            ((taps_hbm, taps_in), (rates_hbm, rates_in), (gains_hbm, gains_in), (skip_hbm, skip_ref))
        )
    ]
    w_copy = pltpu.make_async_copy(w_ref, weights, w_sem)

    barrier = pltpu.get_barrier_semaphore()

    def greet_line(d):
        pl.semaphore_signal(
            barrier, inc=1, device_id=(lax.rem(z + d, nz), c), device_id_type=MESH
        )

    def greet_plane(i):
        pl.semaphore_signal(
            barrier, inc=1, device_id=(z, lax.rem(c + i, nc)), device_id_type=MESH
        )

    each(1, nz, greet_line)
    each(1, nc, greet_plane)
    for copy in small:
        copy.start()
    for s in (1, 2, 0):
        load(s).start()
    w_copy.start()
    for copy in small:
        copy.wait()

    for g in range(subs):
        lanes = slice(g * LANES, (g + 1) * LANES)
        rates_ref[pl.ds(g, modes, stride=subs), :] = rates_in[:, lanes]
        gains_ref[pl.ds(g, modes, stride=subs), :] = gains_in[:, lanes]
        for s in range(3):
            taps_ref[pl.ds(s * width * subs + g, width, stride=subs), :] = taps_in[s, :, lanes]

    pl.semaphore_wait(barrier, nc + nz - 2)

    rim_copy = remote(
        feat_hbm.at[:, pl.ds(tokens - RIM, RIM), :], rim, rim_send, rim_recv,
        (lax.rem(z + 1, nz), c),
    )

    @pl.when(z < nz - 1)
    def _():
        rim_copy.start()

    def unpack(s):
        load(s).wait()
        for g in range(subs):
            wide[s, pl.ds(HEAD * subs + g, tokens, stride=subs), :] = feat_ref[
                s, :, g * LANES : (g + 1) * LANES
            ].astype(jnp.float32)

    unpack(1)
    unpack(2)

    @pl.when(z > 0)
    def _():
        rim_copy.wait_recv()
        for s in range(3):
            for g in range(subs):
                part = rim[s, :, g * LANES : (g + 1) * LANES].astype(jnp.float32)
                wide[s, pl.ds(g, HEAD, stride=subs), :] = part[RIM - HEAD :, :]

    @pl.when(z == 0)
    def _():
        wide[:, pl.ds(0, HEAD * subs), :] = jnp.zeros((3, HEAD * subs, LANES), jnp.float32)

    def at(n):
        return pl.ds(n * subs, subs)

    def token(t):
        return pl.ds(pl.multiple_of(t * subs, subs), subs)

    def featured(s, t, weights):
        value = weights[0] * wide[s, token(t + HEAD), :]
        for j in range(1, width):
            value = value + weights[j] * wide[s, token(t + HEAD - j), :]
        return rounded(value)

    def taps_of(s):
        return [taps_ref[at(s * width + j), :] for j in range(width)]

    decay = [jnp.exp(-rates_ref[at(n), :]) for n in range(modes)]
    taps_1, taps_2 = taps_of(1), taps_of(2)

    def first(i, carry):
        carry = list(carry)
        for u in range(UNROLL):
            t = i * UNROLL + u
            value = rounded(featured(1, t, taps_1) * featured(2, t, taps_2))
            product[token(t), :] = value
            carry = [k * m + value for k, m in zip(decay, carry)]
        return tuple(carry)

    zero = jnp.zeros((subs, LANES), jnp.float32)
    ends = lax.fori_loop(0, tokens // UNROLL, first, (zero,) * modes)
    for n in range(modes):
        total[at(n), :] = ends[n]

    def pass_on(d):
        @pl.when(z + d < nz)
        def _():
            remote(
                total, states.at[d - 1], state_send.at[d - 1], state_recv.at[d - 1],
                (lax.rem(z + d, nz), c),
            ).start()

    each(1, nz, pass_on)

    unpack(0)
    taps_0 = taps_of(0)

    def second(i, carry):
        for u in range(UNROLL):
            t = i * UNROLL + u
            query[token(t), :] = featured(0, t, taps_0)
        return carry

    lax.fori_loop(0, tokens // UNROLL, second, 0)

    def arrive(d):
        @pl.when(z >= d)
        def _():
            remote(
                total, states.at[d - 1], state_send.at[d - 1], state_recv.at[d - 1],
                (lax.rem(z + d, nz), c),
            ).wait_recv()

        @pl.when(z < d)
        def _():
            states[d - 1] = jnp.zeros((modes * subs, LANES), jnp.float32)

    each(1, nz, arrive)

    incoming = []
    for n in range(modes):
        span = jnp.exp(-rates_ref[at(n), :] * float(tokens))
        value = states[nz - 2, at(n), :]
        for d in range(nz - 2, 0, -1):
            value = value * span + states[d - 1, at(n), :]
        incoming.append(value)

    gains = [gains_ref[at(n), :] for n in range(modes)]
    skip = skip_ref[...]

    def scatter(j):
        return remote(g_ref.at[j], stage.at[c], a_send.at[j], a_recv.at[c], (z, j))

    def portion(j, carry):
        def third(i, carry):
            carry = list(carry)
            for u in range(UNROLL):
                t = j * rows + i * UNROLL + u
                value = product[token(t), :]
                carry = [k * m + value for k, m in zip(decay, carry)]
                conv = added([g * m for g, m in zip(gains, carry)] + [skip * value])
                gated[token(i * UNROLL + u), :] = query[token(t), :] * conv
            return tuple(carry)

        carry = lax.fori_loop(0, rows // UNROLL, third, carry)
        for g in range(subs):
            g_ref[j, :, g * LANES : (g + 1) * LANES] = gated[
                pl.ds(g, rows, stride=subs), :
            ].astype(jnp.bfloat16)

        @pl.when(j != c)
        def _():
            scatter(j).start()

        @pl.when(j == c)
        def _():
            pltpu.make_async_copy(g_ref.at[c], stage.at[c], a_recv.at[c]).start()

        return carry

    lax.fori_loop(0, nc, portion, tuple(incoming))

    edges = jnp.minimum(z, nz - 1 - z)

    def plane(s):
        far = (nz - 1 - s // 2, s // 2)
        paired = jnp.where(2 * z < nz - 1, far[s % 2], far[1 - s % 2])
        single = jnp.where(2 * z < nz - 1, nz - 1 - s + edges, s - edges)
        return jnp.where(s < 2 * edges, paired, single)

    def along(s):
        q = plane(s)
        src = stage.at[pl.ds(q * fold, fold)]
        dst = blocks.at[z, :, c]
        if s == nz - 1:
            return pltpu.make_async_copy(src, dst, b_recv.at[z])
        return remote(src, dst, b_send.at[s], b_recv.at[z], (q, c))

    def send_along():
        for s in range(nz):
            for m in range(fold):
                k = plane(s) * fold + m
                pltpu.make_async_copy(g_ref.at[0], stage.at[k], a_recv.at[k]).wait()
            along(s).start()

    def piece(k, j):
        return blocks.at[k, :, j]

    def spread(s, i):
        k = plane(s)
        to = lax.rem(chip + i, chips) * 2 + core
        return remote(piece(k, c), piece(k, c), s_send.at[s, i], s_recv.at[k, chip], (z, to))

    def hand(s, i):
        k = plane(s)
        p = lax.rem(chip + i, chips)
        j = p * 2 + core
        return remote(piece(k, j), piece(k, j), m_send.at[s, i], m_recv.at[k, p], (z, mate))

    def span(h):
        return pl.ds(h * (tokens // CHUNKS), tokens // CHUNKS)

    def back(s, h):
        k = plane(s)
        up = k > z
        to = jnp.where(up, z + 1, z - 1)
        slot = jnp.where(k == z - 1, nz, k)
        return remote(
            sent.at[s, span(h)], taken.at[slot, span(h)], p_send.at[s, h], p_recv.at[slot, h], (to, c)
        )

    def arrived(slot, h):
        there = taken.at[slot, span(h)]
        pltpu.make_async_copy(there, there, p_recv.at[slot, h]).wait()

    def over(h, body):
        each_rows = 32
        base = h * (tokens // CHUNKS)

        def go(i):
            body(pl.ds(pl.multiple_of(base + i * each_rows, each_rows), each_rows))

        pl.loop(0, tokens // CHUNKS // each_rows)(go)

    def multiply(s):
        k = plane(s)

        def strip(i):
            cols = pl.ds(pl.multiple_of(i * tile, tile), tile)
            value = jnp.zeros((tokens, tile), jnp.float32)
            for m in range(fold):
                left = blocks[k, m]
                if rows % 16:
                    left = left.astype(jnp.float32).reshape(tokens, chans).astype(jnp.bfloat16)
                else:
                    left = left.reshape(tokens, chans)
                value = value + jnp.dot(
                    left,
                    weights[m * chans : (m + 1) * chans, cols],
                    preferred_element_type=jnp.float32,
                )
            own[s, :, cols] = value

        pl.loop(0, columns // tile)(strip)

    def begin(s):
        def body(rows_at):
            sent[s, rows_at, :] = own[s, rows_at, :].astype(jnp.bfloat16)

        for h in range(CHUNKS):
            over(h, body)
            back(s, h).start()

    def relay(s):
        k = plane(s)

        def body(rows_at):
            value = own[s, rows_at, :] + taken[k, rows_at, :].astype(jnp.float32)
            sent[s, rows_at, :] = value.astype(jnp.bfloat16)

        for h in range(CHUNKS):
            arrived(k, h)
            over(h, body)
            back(s, h).start()

    def begin_block(s):
        k = plane(s)
        pltpu.make_async_copy(piece(k, c), piece(k, c), b_recv.at[k]).wait()
        each(1, chips, lambda i: spread(s, i).start())
        hand(s, 0).start()

    def forward_block(s):
        k = plane(s)

        def forward(i):
            p = lax.rem(chip + i, chips)
            remote(
                piece(k, c), piece(k, p * 2 + core), s_send.at[s, i], s_recv.at[k, p], (z, mate)
            ).wait_recv()
            hand(s, i).start()

        each(1, chips, forward)

    def collect_block(s):
        k = plane(s)

        def collect(i):
            p = lax.rem(chip + i, chips)
            remote(
                piece(k, c), piece(k, p * 2 + 1 - core), m_send.at[s, i], m_recv.at[k, p], (z, mate)
            ).wait_recv()

        each(0, chips, collect)

    pl.when(edges == 0)(send_along)
    begin_block(0)
    pl.when(edges > 0)(send_along)
    for s in range(nz):
        forward_block(s)
        if s < nz - 1:
            begin_block(s + 1)
        collect_block(s)
        if s == 0:
            w_copy.wait()
        multiply(s)
        if s < nz - 1:
            pl.when(edges == 0)(functools.partial(begin, s))
        if s > 0:
            pl.when(edges > 0)(functools.partial(relay, s - 1))

    def join(slot, h):
        arrived(slot, h)

        def body(rows_at):
            own[nz - 1, rows_at, :] += taken[slot, rows_at, :].astype(jnp.float32)

        over(h, body)

    def finish(rows_at):
        out_ref[rows_at, :] = own[nz - 1, rows_at, :].astype(jnp.bfloat16)

    for h in range(CHUNKS):
        pl.when(z > 0)(functools.partial(join, z, h))
        pl.when(z < nz - 1)(functools.partial(join, nz, h))
        over(h, finish)

    @pl.when(z < nz - 1)
    def _():
        rim_copy.wait_send()

    def leave(d):
        @pl.when(z + d < nz)
        def _():
            remote(
                total, states.at[d - 1], state_send.at[d - 1], state_recv.at[d - 1],
                (lax.rem(z + d, nz), c),
            ).wait_send()

    each(1, nz, leave)
    each(1, nc, lambda i: scatter(lax.rem(c + i, nc)).wait_send())
    for s in range(nz - 1):
        along(s).wait_send()
        for h in range(CHUNKS):
            back(s, h).wait_send()
    for s in range(nz):
        each(1, chips, lambda i: spread(s, i).wait_send())
        each(0, chips, lambda i: hand(s, i).wait_send())


def per_device(nz, nc, features, short_weight, rates, residues, skip, out_weight):
    width = short_weight.shape[1]
    _, tokens, chans = features.shape
    modes = rates.shape[1]
    depth, columns = out_weight.shape
    subs = chans // LANES
    rows = tokens // nc
    fold = nc // nz
    chips = nc // 2
    f32, bf16 = jnp.float32, jnp.bfloat16
    vmem = pl.BlockSpec(memory_space=pltpu.VMEM)
    hbm = pl.BlockSpec(memory_space=pltpu.HBM)
    dma = pltpu.SemaphoreType.DMA

    return pl.pallas_call(
        functools.partial(operator_kernel, nz, nc, modes, width),
        out_shape=jax.ShapeDtypeStruct((tokens, columns), bf16),
        in_specs=[hbm] * 6,
        out_specs=vmem,
        scratch_shapes=[
            pltpu.VMEM((3, tokens, chans), bf16),
            pltpu.VMEM((3, width, chans), f32),
            pltpu.VMEM((modes, chans), f32),
            pltpu.VMEM((modes, chans), f32),
            pltpu.VMEM((subs, LANES), f32),
            pltpu.VMEM((3 * width * subs, LANES), f32),
            pltpu.VMEM((modes * subs, LANES), f32),
            pltpu.VMEM((modes * subs, LANES), f32),
            pltpu.VMEM((3, RIM, chans), bf16),
            pltpu.VMEM((3, (tokens + HEAD) * subs, LANES), f32),
            pltpu.VMEM((tokens * subs, LANES), f32),
            pltpu.VMEM((tokens * subs, LANES), f32),
            pltpu.VMEM((rows * subs, LANES), f32),
            pltpu.VMEM((modes * subs, LANES), f32),
            pltpu.VMEM((nz - 1, modes * subs, LANES), f32),
            pltpu.VMEM((nc, rows, chans), bf16),
            pltpu.VMEM((depth, columns), bf16),
            pltpu.VMEM((nc, rows, chans), bf16),
            pltpu.VMEM((nz, fold, nc, rows, chans), bf16),
            pltpu.VMEM((nz - 1, tokens, columns), bf16),
            pltpu.VMEM((nz + 1, tokens, columns), bf16),
            pltpu.VMEM((nz, tokens, columns), f32),
            dma((3,)), dma, dma, dma((nz - 1,)), dma((nz - 1,)), dma((4,)),
            dma,
            dma((nc,)), dma((nc,)),
            dma((nz,)), dma((nz,)),
            dma((nz, chips)), dma((nz, chips)),
            dma((nz, chips)), dma((nz, chips)),
            dma((nz - 1, CHUNKS)), dma((nz + 1, CHUNKS)),
        ],
        compiler_params=pltpu.CompilerParams(
            collective_id=0, has_side_effects=True, vmem_limit_bytes=62 * 2**20
        ),
        name="operator",
    )(features, short_weight, rates.T, residues.T, skip.reshape(subs, LANES), out_weight)


def solution(mesh):
    return jax.shard_map(
        functools.partial(per_device, mesh.shape["ctx"], mesh.shape["ch"]),
        mesh=mesh,
        in_specs=(
            P(None, "ctx", "ch"),
            P(None, None, "ch"),
            P("ch", None),
            P("ch", None),
            P("ch"),
            P("ctx", "ch"),
        ),
        out_specs=P("ctx", "ch"),
        check_vma=False,
    )
```
